32 devices in a mesh: pool: 4 (over y, core), col: 8 (over z, x).
Axes of the slice: x: 2, y: 2, z: 4, core: 2. Of those that a mesh axis runs over, the one named last changes fastest.
Arguments:
- pair_matrix: bfloat16 [1024, 12288], P('pool', 'col'), may hold values from -1.1953125 to 1.1953125
- band_energy: float32 [4, 4, 4096], P('pool'), may hold values from -2 to 2
- occupation: int32 [4, 4, 4096], P('pool'), may hold values 0 or 1
- pair_first: int32 [4, 256], P('pool'), may hold values from 0 to 4095
- pair_second: int32 [4, 256], P('pool'), may hold values from 0 to 4095
- pair_kpoint: int32 [4, 256], P('pool'), may hold values from 0 to 3
Outputs:
- chi_zero: float32 [12288, 12288], P('pool', 'col')
The draws below stay inside these ranges and needn't reach their ends.
All inputs are finite; a program needn't handle non-finite values. No bound on the sum of `occupation` on one device may be relied on, other than what follows from the above.
Results may differ from the reference program's by a relative error of at most 0.012.
Values may be sent and summed in bfloat16 or wider, within the bound.
A program may use at most 64 MiB of HBM per device.

```python
import jax
import jax.numpy as jnp
from jax import lax

NG = 12288
NBANDS = 4096
KPTS = 4
PAIRS = 256
PAIRS_ALL = 1024
N_POOL = 4


def plant(entries, key, least, largest):
    longest = entries.shape.index(max(entries.shape))
    spots = []
    for shift in (0, 1):
        where = [jax.random.randint(jax.random.fold_in(key, axis), (), 0, length) for axis, length in enumerate(entries.shape)]
        where[longest] = (where[longest] + shift) % entries.shape[longest]
        spots.append(tuple(where))
    return entries.at[spots[0]].set(least).at[spots[1]].set(largest)


def block_scale(own_key, extent, cuts, low, largest):
    factor_of = 1.0
    for axis_at, parts in cuts:
        steps = jax.random.uniform(jax.random.fold_in(jax.random.fold_in(own_key, 6), axis_at), (parts,), jnp.float32, low / len(cuts), largest / len(cuts))
        factor_of = factor_of * jnp.repeat(jnp.exp(steps), extent[axis_at] // parts).reshape((-1,) + (1,) * (len(extent) - 1 - axis_at))
    return factor_of


def scatter_about(key, extent, spread, reach, pieces=(), kind=jnp.bfloat16):
    loudness = block_scale(key, extent, pieces, -0.22, 0.18) if pieces else 1.0
    array = jax.random.normal(key, extent, jnp.float32) * spread * loudness
    return jnp.minimum(jnp.maximum(array, -reach), reach).astype(kind)


def setup_inputs(seed: int = 0) -> dict:
    streams_of = jax.random.split(jax.random.key(seed), 7)
    pair_matrix = scatter_about(streams_of[0], (PAIRS_ALL, NG), 0.2, 1.1953125, ((0, 4), (1, 8)))
    band_energy = jnp.clip(jax.random.uniform(streams_of[1], (N_POOL, KPTS, NBANDS), jnp.float32, -2.0, 2.0) * block_scale(streams_of[1], (N_POOL, KPTS, NBANDS), ((0, 4),), -0.4, 0.0), -2.0, 2.0)
    occupation = plant((jax.random.randint(streams_of[2], (N_POOL, KPTS, NBANDS), 0, 2) < 1).astype(jnp.int32), jax.random.fold_in(streams_of[2], 1), 0, 1)
    pair_first = plant(jax.random.randint(streams_of[3], (N_POOL, PAIRS), 0, NBANDS), jax.random.fold_in(streams_of[3], 1), 0, NBANDS - 1).astype(jnp.int32)
    pair_second = plant(jax.random.randint(streams_of[4], (N_POOL, PAIRS), 0, NBANDS), jax.random.fold_in(streams_of[4], 1), 0, NBANDS - 1).astype(jnp.int32)
    pair_kpoint = plant(jax.random.randint(streams_of[5], (N_POOL, PAIRS), 0, KPTS), jax.random.fold_in(streams_of[5], 1), 0, KPTS - 1).astype(jnp.int32)
    return dict(pair_matrix=pair_matrix, band_energy=band_energy, occupation=occupation, pair_first=pair_first, pair_second=pair_second, pair_kpoint=pair_kpoint)


def pool_weight(energy, occupied, first, second, kpoint):
    flat_energy = energy.reshape(-1)
    flat_occupied = occupied.reshape(-1).astype(jnp.float32)
    index_first = (kpoint * NBANDS + first).astype(jnp.int32)
    index_second = (kpoint * NBANDS + second).astype(jnp.int32)
    gap = jnp.abs(jnp.take(flat_energy, index_second) - jnp.take(flat_energy, index_first))
    filled = jnp.take(flat_occupied, index_first) - jnp.take(flat_occupied, index_second)
    return 2.0 * filled / (1.0 + gap)


def reference(pair_matrix, band_energy, occupation, pair_first, pair_second, pair_kpoint):
    total = jnp.zeros((NG, NG), jnp.float32)
    for pool_index in range(N_POOL):
        weight = pool_weight(band_energy[pool_index], occupation[pool_index], pair_first[pool_index], pair_second[pool_index], pair_kpoint[pool_index])
        block = pair_matrix[pool_index * PAIRS:(pool_index + 1) * PAIRS]
        scaled = (block.astype(jnp.float32) * weight[:, None]).astype(jnp.bfloat16)
        part = lax.dot_general(block, scaled, (((0,), (0,)), ((), ())), preferred_element_type=jnp.float32)
        total = total + part.astype(jnp.bfloat16).astype(jnp.float32)
    return total
```

```python
import functools

import jax
import jax.numpy as jnp
from jax import lax
from jax.experimental import pallas as pl
from jax.experimental.pallas import tpu as pltpu
from jax.sharding import PartitionSpec as P

MESH = pl.DeviceIdType.MESH
LANES = 128
PIECES = 4


def broadcast(value, axis, source):
    kept = jnp.where(lax.axis_index(axis) == source, value, 0).astype(value.dtype)
    return lax.psum(kept, axis)


def pool_weight(energy, occupied, first, second, kpoint):
    bands = energy.shape[-1]
    flat_energy = energy.reshape(-1)
    flat_occupied = occupied.reshape(-1).astype(jnp.float32)
    index_first = kpoint * bands + first
    index_second = kpoint * bands + second
    gap = jnp.abs(jnp.take(flat_energy, index_second) - jnp.take(flat_energy, index_first))
    filled = jnp.take(flat_occupied, index_first) - jnp.take(flat_occupied, index_second)
    return 2.0 * filled / (1.0 + gap)


def per_device_any(pair_matrix, band_energy, occupation, pair_first, pair_second, pair_kpoint):
    weight = pool_weight(
        band_energy[0], occupation[0], pair_first[0], pair_second[0], pair_kpoint[0]
    )
    pools = lax.axis_size("pool")
    group = lax.axis_size("col") // pools
    width = pair_matrix.shape[1]
    all_pairs = lax.all_gather(pair_matrix, "pool", axis=0, tiled=True)
    all_weight = lax.all_gather(weight, "pool", axis=0, tiled=True)
    all_scaled = (all_pairs.astype(jnp.float32) * all_weight[:, None]).astype(jnp.bfloat16)
    first_root = lax.axis_index("pool") * group

    def one_panel(step, total):
        panel = broadcast(all_pairs, "col", first_root + step)
        block = lax.dot_general(
            panel, all_scaled, (((0,), (0,)), ((), ())), preferred_element_type=jnp.float32
        )
        return lax.dynamic_update_slice_in_dim(total, block, step * width, 0)

    start_total = jnp.zeros((group * width, width), jnp.float32)
    return lax.fori_loop(0, group, one_panel, start_total)


def lookup(table, high, low):
    n = high.shape[1]
    rows = lax.broadcasted_iota(jnp.int32, (table.shape[0], n), 0)
    chosen = (rows == high).astype(jnp.float32)
    lines = lax.dot_general(
        table,
        chosen,
        (((0,), (0,)), ((), ())),
        precision=lax.Precision.HIGHEST,
        preferred_element_type=jnp.float32,
    )
    lanes = lax.broadcasted_iota(jnp.int32, (table.shape[1], n), 0)
    return jnp.sum(jnp.where(lanes == low, lines, 0.0), axis=0, keepdims=True)


def gather_kernel(
    depth, m_ref, energy_ref, occupied_ref, first_ref, second_ref, kpoint_ref,
    rows_ref, cols_ref, relay_ref, weight_ref,
    energy_table, occupied_table, own_weight,
    own_sem, line_in, relay_in, cross_in, side_in, mate_in, over_in, back_in, w_in,
    line_up, line_down, line_side, relay_up, relay_down, relay_over, cross_side,
    mate_out, over_out, back_out, w_out,
):
    pairs, width = m_ref.shape
    q, c = lax.axis_index("pool"), lax.axis_index("col")
    y, core = q // 2, q % 2
    z, x = c // 2, c % 2
    dest_z, relay_z = q, (q + 2) % 4
    mate = y * 2 + (1 - core)
    over = (1 - y) * 2 + core
    diagonal = (1 - y) * 2 + (1 - core)
    side = z * 2 + (1 - x)
    piece = pairs // PIECES
    count = 2 * PIECES
    half = 2 * pairs

    has_up, has_down = z < depth - 1, z > 0
    at_source, at_relay = z == dest_z, z == relay_z

    barrier = pltpu.get_barrier_semaphore()

    def greet(pool, col):
        pl.semaphore_signal(barrier, inc=1, device_id=(pool, col), device_id_type=MESH)

    greet(mate, c)
    greet(over, c)
    greet(diagonal, c)
    greet(q, side)

    @pl.when(has_up)
    def _():
        greet(q, c + 2)

    @pl.when(has_down)
    def _():
        greet(q, c - 2)

    neighbours = 4 + has_up.astype(jnp.int32) + has_down.astype(jnp.int32)
    pl.semaphore_wait(barrier, neighbours)

    def remote(source, target, send, receive, pool, col):
        return pltpu.make_async_remote_copy(
            src_ref=source, dst_ref=target, send_sem=send, recv_sem=receive,
            device_id=(pool, col), device_id_type=MESH,
        )

    def spot(n):
        return lax.rem(core * PIECES + n, count)

    def col_at(pool, n):
        return cols_ref.at[pl.ds(pl.multiple_of(pool * pairs + n * piece, piece), piece)]

    def row_at(which_x, which_y, n):
        start = pl.multiple_of(which_y * half + spot(n) * piece, piece)
        return rows_ref.at[which_x, pl.ds(start, piece)]

    def relay_at(n):
        return relay_ref.at[pl.ds(pl.multiple_of(spot(n) * piece, piece), piece)]

    def own_at(n):
        return m_ref.at[pl.ds(pl.multiple_of(n * piece, piece), piece)]

    def to_mate(n):
        return remote(own_at(n), col_at(q, n), mate_out.at[n], mate_in.at[n], mate, c)

    def from_mate(n):
        return remote(own_at(n), col_at(mate, n), mate_out.at[n], mate_in.at[n], mate, c)

    def to_over(n):
        return remote(own_at(n), col_at(q, n), over_out.at[n], over_in.at[n], over, c)

    def from_over(n):
        return remote(own_at(n), col_at(over, n), over_out.at[n], over_in.at[n], over, c)

    def to_back(n):
        ref = col_at(over, n)
        return remote(ref, ref, back_out.at[n], back_in.at[n], mate, c)

    def from_back(n):
        ref = col_at(diagonal, n)
        return remote(ref, ref, back_out.at[n], back_in.at[n], mate, c)

    def line(n, step, send):
        ref = row_at(x, y, n)
        return remote(ref, ref, send.at[n], line_in.at[n], q, c + step)

    def relay(n, step, send):
        ref = relay_at(n)
        return remote(ref, ref, send.at[n], relay_in.at[n], q, c + step)

    def relay_cross(n):
        return remote(
            relay_at(n), row_at(x, y, n), relay_over.at[n], cross_in.at[n], over, c
        )

    def line_to_side(n):
        ref = row_at(x, y, n)
        return remote(ref, ref, line_side.at[n], side_in.at[0, n], q, side)

    def cross_to_side(n):
        ref = row_at(x, 1 - y, n)
        return remote(ref, ref, cross_side.at[n], side_in.at[1, n], q, side)

    line_goes_up = has_up & (z >= dest_z)
    line_goes_down = has_down & (z <= dest_z)
    relay_goes_up = has_up & (z >= relay_z)
    relay_goes_down = has_down & (z <= relay_z)

    def line_step(n):
        pltpu.make_async_copy(row_at(x, y, n), row_at(x, y, n), line_in.at[n]).wait()

        @pl.when(line_goes_up)
        def _():
            line(n, 2, line_up).start()

        @pl.when(line_goes_down)
        def _():
            line(n, -2, line_down).start()

        line_to_side(n).start()

    def relay_step(n):
        pltpu.make_async_copy(relay_at(n), relay_at(n), relay_in.at[n]).wait()

        @pl.when(relay_goes_up)
        def _():
            relay(n, 2, relay_up).start()

        @pl.when(relay_goes_down)
        def _():
            relay(n, -2, relay_down).start()

        relay_cross(n).start()

    def cross_step(n):
        ref = row_at(x, 1 - y, n)
        pltpu.make_async_copy(ref, ref, cross_in.at[n]).wait()
        cross_to_side(n).start()

    def loop(times, body):
        def one(n, carry):
            body(n)
            return carry

        lax.fori_loop(0, times, one, 0)

    def begin(n):
        to_mate(n).start()
        pltpu.make_async_copy(own_at(n), col_at(q, n), own_sem.at[n]).start()

        @pl.when(at_source)
        def _():
            pltpu.make_async_copy(own_at(n), row_at(x, y, n), line_in.at[n]).start()

        @pl.when(at_relay)
        def _():
            pltpu.make_async_copy(own_at(n), relay_at(n), relay_in.at[n]).start()

    loop(PIECES, begin)

    def begin_mate(n):
        from_mate(n).wait_recv()

        @pl.when(at_source)
        def _():
            pltpu.make_async_copy(
                col_at(mate, n), row_at(x, y, PIECES + n), line_in.at[PIECES + n]
            ).start()

        @pl.when(at_relay)
        def _():
            pltpu.make_async_copy(
                col_at(mate, n), relay_at(PIECES + n), relay_in.at[PIECES + n]
            ).start()

    @pl.when(at_source)
    def _():
        loop(PIECES, line_step)

    @pl.when(at_relay)
    def _():
        loop(PIECES, relay_step)

    loop(PIECES, begin_mate)

    @pl.when(at_source)
    def _():
        loop(PIECES, lambda n: line_step(PIECES + n))

    @pl.when(at_relay)
    def _():
        loop(PIECES, lambda n: relay_step(PIECES + n))

    loop(PIECES, lambda n: to_over(n).start())

    kpoints, bands = energy_ref.shape[1:]
    for block in range(bands // LANES):
        here = slice(block * LANES, (block + 1) * LANES)
        there = slice(block * kpoints, (block + 1) * kpoints)
        energy_table[there, :] = energy_ref[0, :, here]
        occupied_table[there, :] = occupied_ref[0, :, here].astype(jnp.float32)

    def values(band):
        high = lax.shift_right_logical(band, 7) * kpoints + kpoint_ref[...]
        low = lax.bitwise_and(band, LANES - 1)
        return (
            lookup(energy_table[...], high, low),
            lookup(occupied_table[...], high, low),
        )

    energy_first, filled_first = values(first_ref[...])
    energy_second, filled_second = values(second_ref[...])
    gap = jnp.abs(energy_second - energy_first)
    weight = 2.0 * (filled_first - filled_second) / (1.0 + gap)
    own_weight[...] = jnp.broadcast_to(weight, own_weight.shape)

    others = (mate, over, diagonal)

    def send_weight(n):
        return remote(
            own_weight, weight_ref.at[q], w_out.at[n], w_in.at[n], others[n], c
        )

    keep_weight = pltpu.make_async_copy(own_weight, weight_ref.at[q], own_sem.at[PIECES])
    keep_weight.start()
    for n in range(3):
        send_weight(n).start()

    def through(n):
        @pl.when(jnp.logical_not(at_relay))
        def _():
            relay_step(n)

        @pl.when(jnp.logical_not(at_source))
        def _():
            line_step(n)

        @pl.when(n > 0)
        def _():
            cross_step(n - 1)

    loop(count, through)
    cross_step(count - 1)

    def give_back(n):
        from_over(n).wait_recv()
        to_back(n).start()

    loop(PIECES, give_back)

    def finish(n):
        pltpu.make_async_copy(
            row_at(1 - x, y, n), row_at(1 - x, y, n), side_in.at[0, n]
        ).wait()
        pltpu.make_async_copy(
            row_at(1 - x, 1 - y, n), row_at(1 - x, 1 - y, n), side_in.at[1, n]
        ).wait()

        @pl.when(line_goes_up)
        def _():
            line(n, 2, line_up).wait_send()

        @pl.when(line_goes_down)
        def _():
            line(n, -2, line_down).wait_send()

        @pl.when(relay_goes_up)
        def _():
            relay(n, 2, relay_up).wait_send()

        @pl.when(relay_goes_down)
        def _():
            relay(n, -2, relay_down).wait_send()

        line_to_side(n).wait_send()
        relay_cross(n).wait_send()
        cross_to_side(n).wait_send()

    loop(count, finish)

    def finish_cols(n):
        from_back(n).wait_recv()
        to_mate(n).wait_send()
        to_over(n).wait_send()
        to_back(n).wait_send()
        pltpu.make_async_copy(own_at(n), col_at(q, n), own_sem.at[n]).wait()

    loop(PIECES, finish_cols)
    keep_weight.wait()
    for n in range(3):
        send_weight(n).wait()


def gather(pair_matrix, band_energy, occupation, pair_first, pair_second, pair_kpoint, depth):
    pairs, width = pair_matrix.shape
    kpoints, bands = band_energy.shape[1:]
    lines = kpoints * bands // LANES
    count = 2 * PIECES
    pools = lax.axis_size("pool")
    dma = pltpu.SemaphoreType.DMA
    anywhere = pl.BlockSpec(memory_space=pl.ANY)
    vmem = pl.BlockSpec(memory_space=pltpu.VMEM)
    return pl.pallas_call(
        functools.partial(gather_kernel, depth),
        out_shape=(
            jax.ShapeDtypeStruct((2, pools * pairs, width), jnp.bfloat16),
            jax.ShapeDtypeStruct((pools * pairs, width), jnp.bfloat16),
            jax.ShapeDtypeStruct((2 * pairs, width), jnp.bfloat16),
            jax.ShapeDtypeStruct((pools, 8, pairs), jnp.float32),
        ),
        in_specs=[anywhere] + [vmem] * 5,
        out_specs=(anywhere,) * 4,
        scratch_shapes=[
            pltpu.VMEM((lines, LANES), jnp.float32),
            pltpu.VMEM((lines, LANES), jnp.float32),
            pltpu.VMEM((8, pairs), jnp.float32),
            dma((PIECES + 1,)),
            dma((count,)), dma((count,)), dma((count,)), dma((2, count)),
            dma((PIECES,)), dma((PIECES,)), dma((PIECES,)), dma((3,)),
            dma((count,)), dma((count,)), dma((count,)),
            dma((count,)), dma((count,)), dma((count,)), dma((count,)),
            dma((PIECES,)), dma((PIECES,)), dma((PIECES,)), dma((3,)),
        ],
        compiler_params=pltpu.CompilerParams(collective_id=0, has_side_effects=True),
    )(pair_matrix, band_energy, occupation, pair_first, pair_second, pair_kpoint)


def multiply_kernel(rows_ref, cols_ref, weight_ref, out_ref, scaled):
    @pl.when((pl.program_id(0) == 0) & (pl.program_id(1) == 0))
    def _():
        pools, _, pairs = weight_ref.shape
        for pool in range(pools):
            here = pl.ds(pool * pairs, pairs)
            column = jnp.transpose(weight_ref[pool])[:, :1]
            scaled[here, :] = (cols_ref[here, :].astype(jnp.float32) * column).astype(jnp.bfloat16)

    out_ref[...] = lax.dot_general(
        rows_ref[0], scaled[...], (((0,), (0,)), ((), ())), preferred_element_type=jnp.float32
    )


def multiply(rows, cols, weight):
    halves, pairs, width = rows.shape
    tile = width // 6
    tiles = width // tile
    return pl.pallas_call(
        multiply_kernel,
        grid=(halves, tiles),
        out_shape=jax.ShapeDtypeStruct((halves * width, width), jnp.float32),
        in_specs=[
            pl.BlockSpec((1, pairs, tile), lambda h, t: (h, 0, t)),
            pl.BlockSpec((pairs, width), lambda h, t: (0, 0)),
            pl.BlockSpec(weight.shape, lambda h, t: (0, 0, 0)),
        ],
        out_specs=pl.BlockSpec((tile, width), lambda h, t: (h * tiles + t, 0)),
        scratch_shapes=[pltpu.VMEM((pairs, width), jnp.bfloat16)],
        compiler_params=pltpu.CompilerParams(vmem_limit_bytes=40 * 1024 * 1024),
    )(rows, cols, weight)


def per_device(pair_matrix, band_energy, occupation, pair_first, pair_second, pair_kpoint):
    pools, cols = lax.axis_size("pool"), lax.axis_size("col")
    if pools != 4 or cols != 2 * pools or pair_matrix.shape[1] % (6 * LANES):
        return per_device_any(
            pair_matrix, band_energy, occupation, pair_first, pair_second, pair_kpoint
        )
    rows, columns, _, weight = gather(
        pair_matrix, band_energy, occupation, pair_first, pair_second, pair_kpoint, cols // 2
    )
    return multiply(rows, columns, weight)


def solution(mesh):
    return jax.shard_map(
        per_device,
        mesh=mesh,
        in_specs=(
            P("pool", "col"),
            P("pool", None, None),
            P("pool", None, None),
            P("pool", None),
            P("pool", None),
            P("pool", None),
        ),
        out_specs=P("pool", "col"),
        check_vma=False,
    )
```

```python
import functools

import jax
import jax.numpy as jnp
from jax import lax
from jax.experimental import pallas as pl
from jax.experimental.pallas import tpu as pltpu
from jax.sharding import PartitionSpec as P

MESH = pl.DeviceIdType.MESH
LANES = 128
PIECES = 8
HOP = 1
CROSS = 2
OVER = 4


def broadcast(value, axis, source):
    kept = jnp.where(lax.axis_index(axis) == source, value, 0).astype(value.dtype)
    return lax.psum(kept, axis)


def pool_weight(energy, occupied, first, second, kpoint):
    bands = energy.shape[-1]
    flat_energy = energy.reshape(-1)
    flat_occupied = occupied.reshape(-1).astype(jnp.float32)
    index_first = kpoint * bands + first
    index_second = kpoint * bands + second
    gap = jnp.abs(jnp.take(flat_energy, index_second) - jnp.take(flat_energy, index_first))
    filled = jnp.take(flat_occupied, index_first) - jnp.take(flat_occupied, index_second)
    return 2.0 * filled / (1.0 + gap)


def per_device_any(pair_matrix, band_energy, occupation, pair_first, pair_second, pair_kpoint):
    weight = pool_weight(
        band_energy[0], occupation[0], pair_first[0], pair_second[0], pair_kpoint[0]
    )
    pools = lax.axis_size("pool")
    group = lax.axis_size("col") // pools
    width = pair_matrix.shape[1]
    all_pairs = lax.all_gather(pair_matrix, "pool", axis=0, tiled=True)
    all_weight = lax.all_gather(weight, "pool", axis=0, tiled=True)
    all_scaled = (all_pairs.astype(jnp.float32) * all_weight[:, None]).astype(jnp.bfloat16)
    first_root = lax.axis_index("pool") * group

    def one_panel(step, total):
        panel = broadcast(all_pairs, "col", first_root + step)
        block = lax.dot_general(
            panel, all_scaled, (((0,), (0,)), ((), ())), preferred_element_type=jnp.float32
        )
        return lax.dynamic_update_slice_in_dim(total, block, step * width, 0)

    start_total = jnp.zeros((group * width, width), jnp.float32)
    return lax.fori_loop(0, group, one_panel, start_total)


def lookup(table, high, low):
    n = high.shape[1]
    rows = lax.broadcasted_iota(jnp.int32, (table.shape[0], n), 0)
    chosen = (rows == high).astype(jnp.float32)
    lines = lax.dot_general(
        table,
        chosen,
        (((0,), (0,)), ((), ())),
        precision=lax.Precision.HIGHEST,
        preferred_element_type=jnp.float32,
    )
    lanes = lax.broadcasted_iota(jnp.int32, (table.shape[1], n), 0)
    return jnp.sum(jnp.where(lanes == low, lines, 0.0), axis=0, keepdims=True)


def gather_kernel(
    depth, m_ref, energy_ref, occupied_ref, first_ref, second_ref, kpoint_ref,
    rows_ref, cols_ref, weight_ref, relay_ref,
    energy_table, occupied_table, own_weight,
    own_sem, line_in, relay_in, cross_in, side_in, mate_in, over_in, back_in, w_in,
    line_up, line_down, line_side, relay_up, relay_down, relay_over, cross_side,
    mate_out, over_out, back_out, w_out,
):
    pairs, width = m_ref.shape
    q, c = lax.axis_index("pool"), lax.axis_index("col")
    y, core = q // 2, q % 2
    z, x = c // 2, c % 2
    dest_z, relay_z = q, (q + 2) % 4
    mate = y * 2 + (1 - core)
    over = (1 - y) * 2 + core
    diagonal = (1 - y) * 2 + (1 - core)
    side = z * 2 + (1 - x)
    piece = pairs // PIECES
    count = 2 * PIECES
    half = 2 * pairs

    has_up, has_down = z < depth - 1, z > 0
    at_source, at_relay = z == dest_z, z == relay_z

    barrier = pltpu.get_barrier_semaphore()

    def greet(pool, col):
        pl.semaphore_signal(barrier, inc=1, device_id=(pool, col), device_id_type=MESH)

    greet(mate, c)
    greet(over, c)
    greet(diagonal, c)
    greet(q, side)

    @pl.when(has_up)
    def _():
        greet(q, c + 2)

    @pl.when(has_down)
    def _():
        greet(q, c - 2)

    neighbours = 4 + has_up.astype(jnp.int32) + has_down.astype(jnp.int32)
    pl.semaphore_wait(barrier, neighbours)

    def remote(source, target, send, receive, pool, col):
        return pltpu.make_async_remote_copy(
            src_ref=source, dst_ref=target, send_sem=send, recv_sem=receive,
            device_id=(pool, col), device_id_type=MESH,
        )

    def spot(n):
        return lax.rem(core * PIECES + n, count)

    def col_at(pool, n):
        return cols_ref.at[pl.ds(pl.multiple_of(pool * pairs + n * piece, piece), piece)]

    def row_at(which_x, which_y, n):
        start = pl.multiple_of(which_y * half + spot(n) * piece, piece)
        return rows_ref.at[which_x, pl.ds(start, piece)]

    def relay_at(n):
        return relay_ref.at[pl.ds(pl.multiple_of(spot(n) * piece, piece), piece)]

    def own_at(n):
        return m_ref.at[pl.ds(pl.multiple_of(n * piece, piece), piece)]

    def to_mate(n):
        return remote(own_at(n), col_at(q, n), mate_out.at[n], mate_in.at[n], mate, c)

    def from_mate(n):
        return remote(own_at(n), col_at(mate, n), mate_out.at[n], mate_in.at[n], mate, c)

    def to_over(n):
        return remote(own_at(n), col_at(q, n), over_out.at[n], over_in.at[n], over, c)

    def from_over(n):
        return remote(own_at(n), col_at(over, n), over_out.at[n], over_in.at[n], over, c)

    def to_back(n):
        ref = col_at(over, n)
        return remote(ref, ref, back_out.at[n], back_in.at[n], mate, c)

    def from_back(n):
        ref = col_at(diagonal, n)
        return remote(ref, ref, back_out.at[n], back_in.at[n], mate, c)

    def line(n, step, send):
        ref = row_at(x, y, n)
        return remote(ref, ref, send.at[n], line_in.at[n], q, c + step)

    def relay(n, step, send):
        ref = relay_at(n)
        return remote(ref, ref, send.at[n], relay_in.at[n], q, c + step)

    def relay_cross(n):
        return remote(
            relay_at(n), row_at(x, y, n), relay_over.at[n], cross_in.at[n], over, c
        )

    def line_to_side(n):
        ref = row_at(x, y, n)
        return remote(ref, ref, line_side.at[n], side_in.at[0, n], q, side)

    def cross_to_side(n):
        ref = row_at(x, 1 - y, n)
        return remote(ref, ref, cross_side.at[n], side_in.at[1, n], q, side)

    line_goes_up = has_up & (z >= dest_z)
    line_goes_down = has_down & (z <= dest_z)
    relay_goes_up = has_up & (z >= relay_z)
    relay_goes_down = has_down & (z <= relay_z)

    def line_step(n):
        pltpu.make_async_copy(row_at(x, y, n), row_at(x, y, n), line_in.at[n]).wait()

        @pl.when(line_goes_up)
        def _():
            line(n, 2, line_up).start()

        @pl.when(line_goes_down)
        def _():
            line(n, -2, line_down).start()

        line_to_side(n).start()

    def relay_step(n):
        pltpu.make_async_copy(relay_at(n), relay_at(n), relay_in.at[n]).wait()

        @pl.when(relay_goes_up)
        def _():
            relay(n, 2, relay_up).start()

        @pl.when(relay_goes_down)
        def _():
            relay(n, -2, relay_down).start()

        relay_cross(n).start()

    def cross_step(n):
        ref = row_at(x, 1 - y, n)
        pltpu.make_async_copy(ref, ref, cross_in.at[n]).wait()
        cross_to_side(n).start()

    def loop(times, body):
        def one(n, carry):
            body(n)
            return carry

        lax.fori_loop(0, times, one, 0)

    def begin(n):
        to_mate(n).start()
        pltpu.make_async_copy(own_at(n), col_at(q, n), own_sem.at[n]).start()

        @pl.when(at_source)
        def _():
            pltpu.make_async_copy(own_at(n), row_at(x, y, n), line_in.at[n]).start()

        @pl.when(at_relay)
        def _():
            pltpu.make_async_copy(own_at(n), relay_at(n), relay_in.at[n]).start()

    loop(PIECES, begin)

    def begin_mate(n):
        from_mate(n).wait_recv()

        @pl.when(at_source)
        def _():
            pltpu.make_async_copy(
                col_at(mate, n), row_at(x, y, PIECES + n), line_in.at[PIECES + n]
            ).start()

        @pl.when(at_relay)
        def _():
            pltpu.make_async_copy(
                col_at(mate, n), relay_at(PIECES + n), relay_in.at[PIECES + n]
            ).start()

    @pl.when(at_source)
    def _():
        loop(PIECES, line_step)

    @pl.when(at_relay)
    def _():
        loop(PIECES, relay_step)

    loop(PIECES, begin_mate)

    @pl.when(at_source)
    def _():
        loop(PIECES, lambda n: line_step(PIECES + n))

    @pl.when(at_relay)
    def _():
        loop(PIECES, lambda n: relay_step(PIECES + n))


    kpoints, bands = energy_ref.shape[1:]
    for block in range(bands // LANES):
        here = slice(block * LANES, (block + 1) * LANES)
        there = slice(block * kpoints, (block + 1) * kpoints)
        energy_table[there, :] = energy_ref[0, :, here]
        occupied_table[there, :] = occupied_ref[0, :, here].astype(jnp.float32)

    def values(band):
        high = lax.shift_right_logical(band, 7) * kpoints + kpoint_ref[...]
        low = lax.bitwise_and(band, LANES - 1)
        return (
            lookup(energy_table[...], high, low),
            lookup(occupied_table[...], high, low),
        )

    energy_first, filled_first = values(first_ref[...])
    energy_second, filled_second = values(second_ref[...])
    gap = jnp.abs(energy_second - energy_first)
    weight = 2.0 * (filled_first - filled_second) / (1.0 + gap)
    own_weight[...] = jnp.broadcast_to(weight, own_weight.shape)

    others = (mate, over, diagonal)

    def send_weight(n):
        return remote(
            own_weight, weight_ref.at[q], w_out.at[n], w_in.at[n], others[n], c
        )

    keep_weight = pltpu.make_async_copy(own_weight, weight_ref.at[q], own_sem.at[PIECES])
    keep_weight.start()
    for n in range(3):
        send_weight(n).start()

    line_late = HOP * jnp.abs(z - dest_z)
    relay_late = HOP * jnp.abs(z - relay_z)
    cross_late = line_late + CROSS

    def through(t):
        n_relay, n_line, n_cross = t - relay_late, t - line_late, t - cross_late
        n_over = t - OVER

        @pl.when((z != relay_z) & (n_relay >= 0) & (n_relay < count))
        def _():
            relay_step(n_relay)

        @pl.when((z != dest_z) & (n_line >= 0) & (n_line < count))
        def _():
            line_step(n_line)

        @pl.when((n_cross >= 0) & (n_cross < count))
        def _():
            cross_step(n_cross)

        @pl.when((n_over >= 0) & (n_over < PIECES))
        def _():
            to_over(n_over).start()

    loop(count + HOP * (depth - 1) + CROSS, through)

    def give_back(n):
        from_over(n).wait_recv()
        to_back(n).start()

    loop(PIECES, give_back)

    def finish(n):
        pltpu.make_async_copy(
            row_at(1 - x, y, n), row_at(1 - x, y, n), side_in.at[0, n]
        ).wait()
        pltpu.make_async_copy(
            row_at(1 - x, 1 - y, n), row_at(1 - x, 1 - y, n), side_in.at[1, n]
        ).wait()

        @pl.when(line_goes_up)
        def _():
            line(n, 2, line_up).wait_send()

        @pl.when(line_goes_down)
        def _():
            line(n, -2, line_down).wait_send()

        @pl.when(relay_goes_up)
        def _():
            relay(n, 2, relay_up).wait_send()

        @pl.when(relay_goes_down)
        def _():
            relay(n, -2, relay_down).wait_send()

        line_to_side(n).wait_send()
        relay_cross(n).wait_send()
        cross_to_side(n).wait_send()

    loop(count, finish)

    def finish_cols(n):
        from_back(n).wait_recv()
        to_mate(n).wait_send()
        to_over(n).wait_send()
        to_back(n).wait_send()
        pltpu.make_async_copy(own_at(n), col_at(q, n), own_sem.at[n]).wait()

    loop(PIECES, finish_cols)
    keep_weight.wait()
    for n in range(3):
        send_weight(n).wait()


def gather(pair_matrix, band_energy, occupation, pair_first, pair_second, pair_kpoint, depth):
    pairs, width = pair_matrix.shape
    kpoints, bands = band_energy.shape[1:]
    lines = kpoints * bands // LANES
    count = 2 * PIECES
    pools = lax.axis_size("pool")
    dma = pltpu.SemaphoreType.DMA
    vmem = pl.BlockSpec(memory_space=pltpu.VMEM)
    return pl.pallas_call(
        functools.partial(gather_kernel, depth),
        out_shape=(
            jax.ShapeDtypeStruct((2, pools * pairs, width), jnp.bfloat16),
            jax.ShapeDtypeStruct((pools * pairs, width), jnp.bfloat16),
            jax.ShapeDtypeStruct((pools, 8, pairs), jnp.float32),
        ),
        in_specs=[vmem] * 6,
        out_specs=(vmem,) * 3,
        scratch_shapes=[
            pltpu.VMEM((2 * pairs, width), jnp.bfloat16),
            pltpu.VMEM((lines, LANES), jnp.float32),
            pltpu.VMEM((lines, LANES), jnp.float32),
            pltpu.VMEM((8, pairs), jnp.float32),
            dma((PIECES + 1,)),
            dma((count,)), dma((count,)), dma((count,)), dma((2, count)),
            dma((PIECES,)), dma((PIECES,)), dma((PIECES,)), dma((3,)),
            dma((count,)), dma((count,)), dma((count,)),
            dma((count,)), dma((count,)), dma((count,)), dma((count,)),
            dma((PIECES,)), dma((PIECES,)), dma((PIECES,)), dma((3,)),
        ],
        compiler_params=pltpu.CompilerParams(
            collective_id=0, has_side_effects=True, vmem_limit_bytes=32 * 1024 * 1024
        ),
    )(pair_matrix, band_energy, occupation, pair_first, pair_second, pair_kpoint)


def per_device(pair_matrix, band_energy, occupation, pair_first, pair_second, pair_kpoint):
    pools, cols = lax.axis_size("pool"), lax.axis_size("col")
    if pools != 4 or cols != 2 * pools or pair_matrix.shape[1] % (6 * LANES):
        return per_device_any(
            pair_matrix, band_energy, occupation, pair_first, pair_second, pair_kpoint
        )
    rows, columns, weight = gather(
        pair_matrix, band_energy, occupation, pair_first, pair_second, pair_kpoint, cols // 2
    )
    scaled = (
        columns.astype(jnp.float32) * weight[:, 0, :].reshape(-1)[:, None]
    ).astype(jnp.bfloat16)
    product = lax.dot_general(
        rows, scaled, (((1,), (0,)), ((), ())), preferred_element_type=jnp.float32
    )
    return product.reshape(-1, columns.shape[1])


def solution(mesh):
    return jax.shard_map(
        per_device,
        mesh=mesh,
        in_specs=(
            P("pool", "col"),
            P("pool", None, None),
            P("pool", None, None),
            P("pool", None),
            P("pool", None),
            P("pool", None),
        ),
        out_specs=P("pool", "col"),
        check_vma=False,
    )
```
